32 devices in a mesh: fsdp: 8 (over z, x), tensor: 4 (over y, core).
Axes of the slice: x: 2, y: 2, z: 4, core: 2. Of those that a mesh axis runs over, the one named last changes fastest.
Arguments:
- inputs: bfloat16 [16384, 1024], P(('fsdp', 'tensor')), may hold values from -6 to 6
- positions: int32 [16384], P('fsdp'), may hold values from 0 to 1023, as said below
- cotangent: bfloat16 [16384, 1024], P(('fsdp', 'tensor')), may hold values from -6 to 6
- gain_one: bfloat16 [1024], replicated, may hold values from 0.5 to 1.5
- shift_one: bfloat16 [1024], replicated, may hold values from -1.25 to 1.25
- gain_two: bfloat16 [1024], replicated, may hold values from 0.5 to 1.5
- shift_two: bfloat16 [1024], replicated, may hold values from -1.25 to 1.25
- qkv_weight: bfloat16 [1024, 3, 1024], P('fsdp', None, 'tensor'), may hold values from -0.1875 to 0.1875
- qkv_bias: bfloat16 [3, 1024], P(None, 'tensor'), may hold values from -1.25 to 1.25
- dense_weight: bfloat16 [1024, 1024], P('fsdp', 'tensor'), may hold values from -0.75 to 0.75
- fc_weight: bfloat16 [1024, 4096], P('fsdp', 'tensor'), may hold values from -0.1875 to 0.1875
- fc_bias: bfloat16 [4096], P('tensor'), may hold values from -1.25 to 1.25
- out_weight: bfloat16 [1024, 4096], P('fsdp', 'tensor'), may hold values from -0.09375 to 0.09375
- out_bias: bfloat16 [1024], replicated, may hold values from -1.25 to 1.25
Outputs:
- output: bfloat16 [16384, 1024], P(('fsdp', 'tensor'))
- input_grad: float32 [16384, 1024], P(('fsdp', 'tensor'))
- gain_one_grad: float32 [1024], replicated
- shift_one_grad: float32 [1024], replicated
- gain_two_grad: float32 [1024], replicated
- shift_two_grad: float32 [1024], replicated
- qkv_weight_grad: float32 [1024, 3, 1024], P('fsdp', None, 'tensor')
- qkv_bias_grad: float32 [3, 1024], P(None, 'tensor')
- dense_weight_grad: float32 [1024, 1024], P('fsdp', 'tensor')
- fc_weight_grad: float32 [1024, 4096], P('fsdp', 'tensor')
- fc_bias_grad: float32 [4096], P('tensor')
- out_weight_grad: float32 [1024, 4096], P('fsdp', 'tensor')
- out_bias_grad: float32 [1024], replicated
The draws below stay inside these ranges and needn't reach their ends.
Inputs may be any that keep to these rules, and one draw needn't show every extreme that they name: `positions`: within each sequence of 1024 consecutive tokens the ids rise by one from 0 at the sequence's first token and restart at 0 at some tokens; some sequence has no restart.
All inputs are finite; a program needn't handle non-finite values.
Results may differ from the reference program's by a relative error of at most 0.01.
Values may be sent and summed in bfloat16 or wider, within the bound.
A program may use at most 192 MiB of HBM per device.

```python
import jax
import jax.numpy as jnp
from jax import lax

D = 1024
HEADS = 16
FF = 4096
HEAD_DIM = 64
ROTARY = 16
SEQ_LEN = 1024
SEQS_DEV = 2
TOKENS = 16384
N_FSDP = 8


def draw_positions(key, part):
    key = jax.random.fold_in(key, 7)
    mark_key, drawn_key = jax.random.split(key)
    sequence_count = TOKENS // SEQ_LEN
    marks = jax.random.randint(mark_key, (sequence_count, SEQ_LEN), 0, max(SEQ_LEN // 4, 2)) == 0
    drawn_sequence = jax.random.randint(drawn_key, (), 0, sequence_count)
    token_index = jnp.arange(SEQ_LEN, dtype=jnp.int32)
    sequence_index = jnp.arange(sequence_count, dtype=jnp.int32)[:, None]
    marks = marks & (sequence_index != drawn_sequence) | (token_index[None, :] == 0)
    starts = lax.cummax(jnp.where(marks, token_index[None, :], 0), axis=1)
    return (token_index[None, :] - starts).reshape(TOKENS).astype(jnp.int32)


def spiked(array, stream_key, source, target, shards_of, factor):
    owner, partner = [(jnp.arange(array.shape[position]) // (array.shape[position] // shards_of)).reshape([-1 if axis == position else 1 for axis in range(array.ndim)]) for position in (source, target)]
    chosen = jax.random.permutation(stream_key, shards_of)[partner]
    strong = (owner == chosen) | (owner == (partner + shards_of // 2) % shards_of)
    return jnp.where(strong, factor * array, array)


def block_scale(key, dims, cuts, least, high):
    factor_of = 1.0
    for dim, parts in cuts:
        draws = jax.random.uniform(jax.random.fold_in(jax.random.fold_in(key, 6), dim), (parts,), jnp.float32, least / len(cuts), high / len(cuts))
        factor_of = factor_of * jnp.repeat(jnp.exp(draws), dims[dim] // parts).reshape((-1,) + (1,) * (len(dims) - 1 - dim))
    return factor_of


def gaussian(stream_key, extent, scale, bound, cuts=(), kind=jnp.bfloat16):
    factor_of = block_scale(stream_key, extent, cuts, -0.22, 0.18) if cuts else 1.0
    array = jax.random.normal(stream_key, extent, jnp.float32) * scale * factor_of
    return jnp.minimum(jnp.maximum(array, -bound), bound).astype(kind)


def heavy_noise(rng, shape, deviation, reach, cuts, heavy, kind=jnp.bfloat16):
    values = deviation * jax.random.normal(rng, shape, jnp.float32)
    if cuts:
        values = values * block_scale(rng, shape, cuts, -0.22, 0.18)
    return jnp.clip(spiked(values, jax.random.fold_in(rng, 3), *heavy), -reach, reach).astype(kind)


def setup_inputs(seed: int = 0) -> dict:
    splits = jax.random.split(jax.random.key(seed), 15)
    return {
        "inputs": heavy_noise(splits[0], (TOKENS, D), 1.0, 6.0, ((0, 32),), (0, 1, 32, 2.75)),
        "positions": draw_positions(jax.random.fold_in(splits[14], 71), 0),
        "cotangent": heavy_noise(splits[2], (TOKENS, D), 1.0, 6.0, ((0, 32),), (0, 1, 32, 2.75)),
        "gain_one": jnp.clip(1.0 + 0.1 * jax.random.normal(splits[3], (D,), jnp.float32), 0.5, 1.5).astype(jnp.bfloat16),
        "shift_one": gaussian(splits[4], (D,), 0.2, 1.25),
        "gain_two": jnp.clip(1.0 + 0.1 * jax.random.normal(splits[5], (D,), jnp.float32), 0.5, 1.5).astype(jnp.bfloat16),
        "shift_two": gaussian(splits[6], (D,), 0.2, 1.25),
        "qkv_weight": gaussian(splits[7], (D, 3, D), D ** -0.5, 0.1875, ((0, 8), (2, 4))),
        "qkv_bias": gaussian(splits[8], (3, D), 0.2, 1.25, ((1, 4),)),
        "dense_weight": gaussian(splits[9], (D, D), (D // 16) ** -0.5, 0.75, ((0, 8), (1, 4))),
        "fc_weight": gaussian(splits[10], (D, FF), D ** -0.5, 0.1875, ((0, 8), (1, 4))),
        "fc_bias": gaussian(splits[11], (FF,), 0.2, 1.25, ((0, 4),)),
        "out_weight": gaussian(splits[12], (D, FF), FF ** -0.5, 0.09375, ((0, 8), (1, 4))),
        "out_bias": gaussian(splits[13], (D,), 0.2, 1.25),
    }


@jax.custom_vjp
def low(v):
    return lax.optimization_barrier(v.astype(jnp.bfloat16)).astype(jnp.float32)

@jax.custom_vjp
def low_back(v):
    return v

def low_keep(v):
    return (low(v), None)

def low_pass(kept, grad):
    return (grad,)

def back_keep(v):
    return (v, None)

def back_low(kept, grad):
    return (low(grad),)
low.defvjp(low_keep, low_pass)
low_back.defvjp(back_keep, back_low)
highest = lax.Precision.HIGHEST

def norm_rows(rows_in, gain, shift):
    average = lax.optimization_barrier(jnp.mean(rows_in, axis=-1, keepdims=True))
    centred = rows_in - average
    inverse_std = lax.rsqrt(lax.optimization_barrier(jnp.mean(centred * centred, axis=-1, keepdims=True)) + 1e-05)
    return centred * inverse_std * gain + shift

def rotary_tables(position_ids):
    exponents = jnp.arange(0, ROTARY, 2).astype(jnp.float32) / ROTARY
    inverse = 1.0 / 10000.0 ** exponents
    phases = position_ids.astype(jnp.float32)[:, None] * inverse[None, :]
    phases = jnp.concatenate([phases, phases], axis=-1)
    return (jnp.cos(phases)[:, None, :], jnp.sin(phases)[:, None, :])

def rotate_heads(heads_in, cosine_table, sine_table):
    turned = heads_in[..., :ROTARY]
    lower_half = turned[..., :ROTARY // 2]
    upper_half = turned[..., ROTARY // 2:]
    swapped = jnp.concatenate([-upper_half, lower_half], axis=-1)
    return jnp.concatenate([turned * cosine_table + swapped * sine_table, heads_in[..., ROTARY:]], axis=-1)

def attend(seq_block):
    query_heads, key_heads, value_heads = seq_block
    score_scale = HEAD_DIM ** (-0.5)
    scores = low_back(jnp.einsum('qhd,khd->hqk', query_heads, key_heads, precision=highest) * score_scale)
    rows_index = lax.broadcasted_iota(jnp.int32, (SEQ_LEN, SEQ_LEN), 0)
    cols_index = lax.broadcasted_iota(jnp.int32, (SEQ_LEN, SEQ_LEN), 1)
    scores = jnp.where((cols_index <= rows_index)[None], scores, -1e+30)
    chances = low(jax.nn.softmax(scores, axis=-1))
    return jnp.einsum('hqk,khd->qhd', chances, value_heads, precision=highest)

def layer_forward(inputs, weights, cosine_table, sine_table):
    gain_one, shift_one, gain_two, shift_two, qkv_weight, qkv_bias, dense_weight, fc_weight, fc_bias, out_weight, out_bias = weights
    row_count = inputs.shape[0]
    normed_one = low(norm_rows(inputs, gain_one, shift_one))
    normed_two = low(norm_rows(inputs, gain_two, shift_two))
    projected = jnp.einsum('td,dcf->tcf', normed_one, qkv_weight, precision=highest) + qkv_bias
    query_pre = low_back(projected[:, 0]).reshape(row_count, HEADS, HEAD_DIM)
    key_pre = low_back(projected[:, 1]).reshape(row_count, HEADS, HEAD_DIM)
    value_heads = low(low_back(projected[:, 2])).reshape(row_count, HEADS, HEAD_DIM)
    query_heads = low(rotate_heads(query_pre, cosine_table, sine_table))
    key_heads = low(rotate_heads(key_pre, cosine_table, sine_table))
    sequences = row_count // SEQ_LEN
    seq_shape = (sequences, SEQ_LEN, HEADS, HEAD_DIM)
    attended = lax.map(jax.checkpoint(attend), (query_heads.reshape(seq_shape), key_heads.reshape(seq_shape), value_heads.reshape(seq_shape)))
    attended = low_back(low(attended.reshape(row_count, D)))
    attention_part = jnp.dot(attended, dense_weight.T, precision=highest, preferred_element_type=jnp.float32)
    hidden_pre = low_back(jnp.dot(normed_two, fc_weight, precision=highest, preferred_element_type=jnp.float32) + fc_bias)
    hidden_act = low(jax.nn.gelu(hidden_pre, approximate=False))
    mlp_part = jnp.dot(hidden_act, out_weight.T, precision=highest, preferred_element_type=jnp.float32)
    return inputs + attention_part + mlp_part + out_bias

def reference(inputs, positions, cotangent, gain_one, shift_one, gain_two, shift_two, qkv_weight, qkv_bias, dense_weight, fc_weight, fc_bias, out_weight, out_bias):
    weights_in = (gain_one.astype(jnp.float32), shift_one.astype(jnp.float32), gain_two.astype(jnp.float32), shift_two.astype(jnp.float32), qkv_weight.astype(jnp.float32), qkv_bias.astype(jnp.float32), dense_weight.astype(jnp.float32), fc_weight.astype(jnp.float32), fc_bias.astype(jnp.float32), out_weight.astype(jnp.float32), out_bias.astype(jnp.float32))
    group_rows = SEQS_DEV * SEQ_LEN
    inputs_blocks = inputs.astype(jnp.float32).reshape(N_FSDP, group_rows, D)
    position_blocks = positions.astype(jnp.int32).reshape(N_FSDP, group_rows)
    cotangent_blocks = cotangent.astype(jnp.float32).reshape(N_FSDP, group_rows, D)

    def scan_step(running, seq_group):
        rows_in, rows_position, rows_grad = seq_group
        cosine_table, sine_table = rotary_tables(rows_position)

        def forward_only(rows_value, *weights):
            return layer_forward(rows_value, weights, cosine_table, sine_table)
        result, pullback = jax.vjp(forward_only, rows_in, *weights_in)
        gradients = pullback(rows_grad)
        running = tuple((left + right for left, right in zip(running, gradients[1:])))
        return (running, (result.astype(jnp.bfloat16), gradients[0]))
    zero_sums = tuple((jnp.zeros_like(weight) for weight in weights_in))
    totals, (outputs, input_grads) = lax.scan(scan_step, zero_sums, (inputs_blocks, position_blocks, cotangent_blocks))
    return (outputs.reshape(TOKENS, D), input_grads.reshape(TOKENS, D), totals[0], totals[1], totals[2], totals[3], totals[4], totals[5], totals[6], totals[7], totals[8], totals[9], totals[10])
```

```python
from functools import partial

import jax
import jax.numpy as jnp
from jax import lax
from jax.experimental import pallas as pl
from jax.experimental.pallas import tpu as pltpu
from jax.sharding import PartitionSpec as P

HEAD_DIM = 64
ROTARY = 16
SEQ_LEN = 1024
PAIR = 2 * HEAD_DIM
ROWS = 256
F32 = jnp.float32
BF16 = jnp.bfloat16


def dot(a, b, dims):
    return lax.dot_general(a, b, (dims, ((), ())), preferred_element_type=F32)


NN = ((1,), (0,))
NT = ((1,), (1,))
TN = ((0,), (0,))


def row_stats(rows_in):
    average = jnp.mean(rows_in, axis=-1, keepdims=True)
    centred = rows_in - average
    inverse_std = lax.rsqrt(jnp.mean(centred * centred, axis=-1, keepdims=True) + 1e-05)
    return average, inverse_std


def rotary_tables(position_ids):
    half = ROTARY // 2
    exponents = jnp.arange(0, ROTARY, 2).astype(F32) / ROTARY
    inverse = 1.0 / 10000.0**exponents
    phases = position_ids.astype(F32)[:, None] * inverse[None, :]
    cosine, sine = jnp.cos(phases), jnp.sin(phases)
    count = position_ids.shape[0]
    rest = HEAD_DIM - ROTARY
    ones, zeros, gap = jnp.ones((count, rest), F32), jnp.zeros((count, rest), F32), jnp.zeros((count, half), F32)
    keep = jnp.concatenate([cosine, cosine, ones] * 2, axis=1)
    upper = jnp.concatenate([gap, sine, zeros] * 2, axis=1)
    lower = jnp.concatenate([-sine, gap, zeros] * 2, axis=1)
    return keep, upper, lower


def attention_kernel(
    projected, bias, keep, upper, lower, grad_rows, attended, grad_projected, query, key_rows, value, grad_key, grad_value
):
    width = attended.shape[1]
    pair = pl.program_id(1)
    half = ROTARY // 2
    scale = HEAD_DIM ** (-0.5)

    def columns(part):
        return pl.ds(pl.multiple_of(part * width + pair * PAIR, PAIR), PAIR)

    def turn(block):
        return (
            block * keep[...]
            + pltpu.roll(block, half, 1) * upper[...]
            + pltpu.roll(block, PAIR - half, 1) * lower[...]
        )

    def turn_back(block, rows):
        return (
            block * keep[rows, :]
            - pltpu.roll(block, half, 1) * upper[rows, :]
            - pltpu.roll(block, PAIR - half, 1) * lower[rows, :]
        )

    query_all = turn(projected[:, columns(0)] + bias[:, columns(0)]).astype(BF16) * jnp.asarray(scale, BF16)
    key_all = turn(projected[:, columns(1)] + bias[:, columns(1)]).astype(BF16)
    value_all = (projected[:, columns(2)] + bias[:, columns(2)]).astype(BF16)
    for head in range(2):
        part = slice(head * HEAD_DIM, (head + 1) * HEAD_DIM)
        query[head] = query_all[:, part]
        key_rows[head] = key_all[:, part]
        value[head] = value_all[:, part]
    grad_key[...] = jnp.zeros_like(grad_key)
    grad_value[...] = jnp.zeros_like(grad_value)
    row_index = lax.broadcasted_iota(jnp.int32, (ROWS, ROWS), 0)
    col_index = lax.broadcasted_iota(jnp.int32, (ROWS, ROWS), 1)
    below = col_index <= row_index
    length = projected.shape[0]
    for block in range(length // ROWS):
        rows = pl.ds(block * ROWS, ROWS)
        reach = (block + 1) * ROWS
        outs, grads = [], []
        grad_pair = grad_rows[rows, pl.ds(pl.multiple_of(pair * PAIR, PAIR), PAIR)]
        for head in range(2):
            q = query[head, rows, :]
            k = key_rows[head, pl.ds(0, reach), :]
            v = value[head, pl.ds(0, reach), :]
            g = grad_pair[:, head * HEAD_DIM : (head + 1) * HEAD_DIM]
            scores = dot(q, k, NT)
            last = jnp.where(below, scores[:, reach - ROWS :], -1e30)
            scores = last if block == 0 else jnp.concatenate([scores[:, : reach - ROWS], last], axis=1)
            weights = jnp.exp(scores - jnp.max(scores, axis=1, keepdims=True))
            probs = weights * (1.0 / jnp.sum(weights, axis=1, keepdims=True))
            chances = probs.astype(BF16)
            outs.append(dot(chances, v, NN))
            grad_chances = dot(g, v, NT)
            inner = jnp.sum(probs * grad_chances, axis=1, keepdims=True)
            grad_scores = (probs * (grad_chances - inner)).astype(BF16)
            grads.append(dot(grad_scores, k, NN) * scale)
            strip = pl.ds(head * HEAD_DIM, HEAD_DIM)
            grad_value[strip, pl.ds(0, reach)] += dot(g, chances, TN)
            grad_key[strip, pl.ds(0, reach)] += dot(q, grad_scores, TN)
        attended[rows, pl.ds(pl.multiple_of(pair * PAIR, PAIR), PAIR)] = jnp.concatenate(outs, axis=1).astype(BF16)
        grad_projected[rows, columns(0)] = turn_back(jnp.concatenate(grads, axis=1), rows).astype(BF16)
    everything = pl.ds(0, length)
    grad_projected[:, columns(1)] = turn_back(grad_key[...].T, everything).astype(BF16)
    grad_projected[:, columns(2)] = grad_value[...].T.astype(BF16)


def attention(projected, bias, tables, grad_rows):
    group, wide = projected.shape
    width = grad_rows.shape[1]
    sequences = group // SEQ_LEN
    pairs = width // PAIR
    by_seq = lambda size: pl.BlockSpec((SEQ_LEN, size), lambda s, p: (s, 0))
    heads = group // SEQ_LEN * width // HEAD_DIM
    return pl.pallas_call(
        attention_kernel,
        grid=(sequences, pairs),
        in_specs=[by_seq(wide), pl.BlockSpec((1, wide), lambda s, p: (0, 0))] + [by_seq(PAIR)] * 3 + [by_seq(width)],
        out_specs=[by_seq(width), by_seq(wide)],
        out_shape=[jax.ShapeDtypeStruct((group, width), BF16), jax.ShapeDtypeStruct((group, wide), BF16)],
        scratch_shapes=[pltpu.VMEM((2, SEQ_LEN, HEAD_DIM), BF16)] * 3 + [pltpu.VMEM((PAIR, SEQ_LEN), F32)] * 2,
        compiler_params=pltpu.CompilerParams(vmem_limit_bytes=48 * 1024 * 1024),
        cost_estimate=pl.CostEstimate(
            flops=heads * 14 * SEQ_LEN * SEQ_LEN * 256,
            bytes_accessed=group * wide * 8,
            transcendentals=heads * SEQ_LEN * SEQ_LEN,
        ),
        name="attention",
    )(projected, bias, *tables, grad_rows)


def swap(array, axis, bit, size):
    return lax.ppermute(array, axis, [(i, i ^ bit) for i in range(size)])


def gather_tensor(block):
    rows, wide = block.shape
    mine = lax.axis_index("tensor")
    high, core = mine // 2, mine % 2
    far = swap(block, "tensor", 2, 4)
    chips = jnp.where(high == 0, jnp.stack([block, far]), jnp.stack([far, block]))
    other = swap(chips, "tensor", 1, 4)
    whole = jnp.where(core == 0, jnp.stack([chips, other], axis=1), jnp.stack([other, chips], axis=1))
    return whole.reshape(4 * rows, wide)


def scatter_tensor(partial_rows):
    group, wide = partial_rows.shape
    mine = lax.axis_index("tensor")
    high, core = mine // 2, mine % 2
    parts = partial_rows.reshape(2, 2, group // 4, wide)
    sent = lax.dynamic_index_in_dim(parts, 1 - core, 1, keepdims=False).astype(BF16)
    kept = lax.dynamic_index_in_dim(parts, core, 1, keepdims=False)
    got = swap(sent, "tensor", 1, 4)
    far = lax.dynamic_index_in_dim(kept, 1 - high, 0, keepdims=False) + lax.dynamic_index_in_dim(
        got, 1 - high, 0, keepdims=False
    ).astype(F32)
    near = lax.dynamic_index_in_dim(kept, high, 0, keepdims=False) + lax.dynamic_index_in_dim(
        got, high, 0, keepdims=False
    ).astype(F32)
    return near + swap(far.astype(BF16), "tensor", 2, 4).astype(F32)


def shards(
    fsdp_size,
    inputs,
    positions,
    cotangent,
    gain_one,
    shift_one,
    gain_two,
    shift_two,
    qkv_weight,
    qkv_bias,
    dense_weight,
    fc_weight,
    fc_bias,
    out_weight,
    out_bias,
):
    features = inputs.shape[1]
    local = qkv_bias.shape[1]
    gain_first, shift_first = gain_one.astype(F32), shift_one.astype(F32)
    gain_second, shift_second = gain_two.astype(F32), shift_two.astype(F32)

    own = jnp.concatenate([qkv_weight.reshape(qkv_weight.shape[0], -1), dense_weight], axis=1)
    whole_attn = lax.all_gather(own, "fsdp", axis=0, tiled=True)
    whole_fc = lax.all_gather(fc_weight, "fsdp", axis=0, tiled=True)
    whole_out = lax.all_gather(out_weight, "fsdp", axis=0, tiled=True)
    whole_qkv, whole_dense = whole_attn[:, : 3 * local], whole_attn[:, 3 * local :]

    group_inputs = gather_tensor(inputs).astype(F32)
    group_grad = gather_tensor(cotangent)
    average, inverse_std = row_stats(group_inputs)
    standard = (group_inputs - average) * inverse_std
    group_one = (standard * gain_first + shift_first).astype(BF16)
    group_two = (standard * gain_second + shift_second).astype(BF16)
    tables = rotary_tables(positions)

    projected = dot(group_one, whole_qkv, NN)
    grad_attended = dot(group_grad, whole_dense, NN).astype(BF16)
    attended, grad_projected = attention(
        projected, qkv_bias.astype(F32).reshape(1, -1), tables, grad_attended
    )

    hidden_pre = dot(group_two, whole_fc, NN) + fc_bias.astype(F32)
    hidden_act, gelu_pullback = jax.vjp(partial(jax.nn.gelu, approximate=False), hidden_pre)
    hidden_act = hidden_act.astype(BF16)
    grad_act = dot(group_grad, whole_out, NN)
    grad_hidden = gelu_pullback(grad_act)[0].astype(BF16)

    grad_out = dot(group_grad, hidden_act, TN)
    shard_out = lax.psum_scatter(grad_out.astype(BF16), "fsdp", scatter_dimension=0, tiled=True).astype(F32)
    grad_fc = dot(group_two, grad_hidden, TN)
    shard_fc = lax.psum_scatter(grad_fc.astype(BF16), "fsdp", scatter_dimension=0, tiled=True).astype(F32)
    back_two = dot(grad_hidden, whole_fc, NT)

    branches = dot(attended, whole_dense, NT) + dot(hidden_act, whole_out, NT)
    branch_rows = scatter_tensor(branches)
    inputs_wide = inputs.astype(F32)
    output = (inputs_wide + branch_rows + out_bias.astype(F32)).astype(BF16)

    grad_attn = jnp.concatenate([dot(group_one, grad_projected, TN), dot(group_grad, attended, TN)], axis=1)
    shard_attn = lax.psum_scatter(grad_attn.astype(BF16), "fsdp", scatter_dimension=0, tiled=True).astype(F32)

    back_one = dot(grad_projected, whole_qkv, NT)
    slopes = scatter_tensor(back_one * gain_first + back_two * gain_second)
    own_average, own_inverse = row_stats(inputs_wide)
    own_standard = (inputs_wide - own_average) * own_inverse
    cotangent_wide = cotangent.astype(F32)
    grad_inputs = cotangent_wide + own_inverse * (
        slopes
        - jnp.mean(slopes, axis=-1, keepdims=True)
        - own_standard * jnp.mean(slopes * own_standard, axis=-1, keepdims=True)
    )

    sums = jnp.concatenate(
        [
            jnp.sum(back_one * standard, axis=0),
            jnp.sum(back_one, axis=0),
            jnp.sum(back_two * standard, axis=0),
            jnp.sum(back_two, axis=0),
            jnp.sum(cotangent_wide, axis=0),
        ]
    )
    for bit in (1, 2):
        sums = sums + swap(sums, "tensor", bit, 4)
    sums = jnp.concatenate(
        [sums, jnp.sum(grad_projected.astype(F32), axis=0), jnp.sum(grad_hidden.astype(F32), axis=0)]
    )
    bit = 1
    while bit < fsdp_size:
        sums = sums + swap(sums, "fsdp", bit, fsdp_size)
        bit *= 2
    small = [sums[i * features : (i + 1) * features] for i in range(5)]
    rest = sums[5 * features :]
    return (
        output,
        grad_inputs,
        small[0],
        small[1],
        small[2],
        small[3],
        shard_attn[:, : 3 * local].reshape(-1, 3, local),
        rest[: 3 * local].reshape(3, local),
        shard_attn[:, 3 * local :],
        shard_fc,
        rest[3 * local :],
        shard_out,
        small[4],
    )


def solution(mesh):
    placed = (
        P(("fsdp", "tensor"), None),
        P("fsdp"),
        P(("fsdp", "tensor"), None),
        P(),
        P(),
        P(),
        P(),
        P("fsdp", None, "tensor"),
        P(None, "tensor"),
        P("fsdp", "tensor"),
        P("fsdp", "tensor"),
        P("tensor"),
        P("fsdp", "tensor"),
        P(),
    )
    return jax.shard_map(
        partial(shards, mesh.shape["fsdp"]),
        mesh=mesh,
        in_specs=placed,
        out_specs=(
            P(("fsdp", "tensor"), None),
            P(("fsdp", "tensor"), None),
            P(),
            P(),
            P(),
            P(),
            P("fsdp", None, "tensor"),
            P(None, "tensor"),
            P("fsdp", "tensor"),
            P("fsdp", "tensor"),
            P("tensor"),
            P("fsdp", "tensor"),
            P(),
        ),
        check_vma=False,
    )
```
